32 devices in a mesh: dp: 8 (over y, x, core), seq: 4 (over z).
Axes of the slice: x: 2, y: 2, z: 4, core: 2. Of those that a mesh axis runs over, the one named last changes fastest.
Arguments:
- hidden_states: bfloat16 [4096, 5120], P(('dp', 'seq')), may hold values from -6 to 6
- value_weight: bfloat16 [5120, 1024], P('dp'), may hold values from -0.078125 to 0.078125
- query_states: bfloat16 [4096, 8192], P(('dp', 'seq')), may hold values from -140 to 140
- key_states: bfloat16 [4096, 1024], P(('dp', 'seq')), may hold values from -4.5 to 4.5
- cotangent: bfloat16 [4096, 8192], P(('dp', 'seq')), may hold values from -6 to 6
- lengths: int32 [8, 8], P('dp'), may hold values from 1 to 256, 512 in all within a row
Outputs:
- attention_out: bfloat16 [4096, 8192], P(('dp', 'seq'))
- query_grad: bfloat16 [4096, 8192], P(('dp', 'seq'))
- key_grad: bfloat16 [4096, 1024], P(('dp', 'seq'))
- input_grad: bfloat16 [4096, 5120], P(('dp', 'seq'))
- value_weight_grad: float32 [5120, 1024], P('dp')
The draws below stay inside these ranges and needn't reach their ends.
Inputs may be any that keep to these rules, and one draw needn't show every extreme that they name: Row g lists the 8 response lengths of group g's pack; they sum to 512 and the longest is 256.
All inputs are finite; a program needn't handle non-finite values.
Results may differ from the reference program's by a relative error of at most 0.04.
Values may be sent and summed in bfloat16 or wider, within the bound.
A program may use at most 256 MiB of HBM per device.

```python
import math
import jax
import jax.numpy as jnp
import numpy as np
from jax import lax

D = 5120
HEADS = 64
KV_HEADS = 8
HEAD_DIM = 128
DOCS = 8
PACK = 512
MOST = 256
TOKENS = 4096
N_DP = 8


def shared_keys(key):
    return jnp.clip(jax.random.normal(key, (TOKENS, KV_HEADS * HEAD_DIM), jnp.float32), -4.0, 4.0)


def draw_key_states(key, part):
    base = shared_keys(key)
    return base.astype(jnp.bfloat16)


def draw_query_states(key, part):
    key = jax.random.fold_in(key, 7)
    first_key = jax.random.fold_in(key, 0)
    drawn = jnp.clip(jax.random.normal(first_key, (TOKENS, HEADS * HEAD_DIM), jnp.float32), -4.0, 4.0)
    return drawn.astype(jnp.bfloat16)


def raised(drawn, key, source, target, blocks, factor):
    def block_of(dim):
        return (jnp.arange(drawn.shape[dim]) // (drawn.shape[dim] // blocks)).reshape((-1,) + (1,) * (drawn.ndim - 1 - dim))

    near = jax.random.permutation(key, blocks)[block_of(target)]
    other_side = (block_of(target) + blocks // 2) % blocks
    return jnp.where((block_of(source) == near) | (block_of(source) == other_side), factor * drawn, drawn)


def block_levels(own_key, extent, cuts, smallest, largest):
    def one(dim, shards_of):
        steps = jax.random.uniform(jax.random.fold_in(jax.random.fold_in(own_key, 6), dim), (shards_of,), jnp.float32, smallest / len(cuts), largest / len(cuts))
        return jnp.repeat(jnp.exp(steps), extent[dim] // shards_of).reshape((-1,) + (1,) * (len(extent) - dim - 1))

    gain = one(*cuts[0])
    for cut in cuts[1:]:
        gain = gain * one(*cut)
    return gain


def profile(number_of, total, most, skew):
    portions = [(1 << 20) // math.isqrt(standing ** skew) + 1 for standing in range(2, number_of + 1)]
    spare, counts = total - most - (number_of - 1), [1] * (number_of - 1)
    while spare > 0:
        movable = [i for i in range(number_of - 1) if counts[i] < most]
        whole, left = sum([portions[i] for i in movable]), spare
        for i in movable:
            more = min(most - counts[i], max(1, left * portions[i] // whole), spare)
            counts[i] = counts[i] + more
            spare = spare - more
    return np.array([most] + counts)


def ragged_sizes(stream_key, number_of, total, bound, skew):
    if number_of == 2:
        one = jax.random.randint(stream_key, (), max(1, total - bound), min(bound, total - 1) + 1)
        return jnp.stack([one, total - one])
    tallies = jnp.asarray(profile(number_of, total, bound, skew), jnp.int32)
    couples = (number_of - 1) // 2
    source_of, taker = tallies[1:1 + 2 * couples:2], tallies[2:2 + 2 * couples:2]
    margin = jnp.minimum(source_of - 1, bound - taker)
    passed = jax.random.randint(jax.random.fold_in(stream_key, 1), (couples,), 0, 1 << 20) % (margin + 1)
    tallies = tallies.at[1:1 + 2 * couples:2].set(source_of - passed).at[2:2 + 2 * couples:2].set(taker + passed)
    return tallies[jax.random.permutation(jax.random.fold_in(stream_key, 2), number_of)]


def gaussian(rng, dims, width, reach, cuts=(), kind=jnp.bfloat16):
    level = block_levels(rng, dims, cuts, -0.22, 0.18) if cuts else 1.0
    values = jax.random.normal(rng, dims, jnp.float32) * width * level
    return jnp.minimum(jnp.maximum(values, -reach), reach).astype(kind)


def heavy_noise(rng, dims, spread, bound, cuts, heavy, kind=jnp.bfloat16):
    drawn = spread * jax.random.normal(rng, dims, jnp.float32)
    if cuts:
        drawn = drawn * block_levels(rng, dims, cuts, -0.22, 0.18)
    return jnp.clip(raised(drawn, jax.random.fold_in(rng, 3), *heavy), -bound, bound).astype(kind)


def setup_inputs(seed: int = 0) -> dict:
    arg_keys = jax.random.split(jax.random.key(seed), 7)
    return {
        "hidden_states": heavy_noise(arg_keys[0], (TOKENS, D), 1.0, 6.0, ((0, 32),), (0, 1, 32, 2.75)),
        "value_weight": gaussian(arg_keys[1], (D, KV_HEADS * HEAD_DIM), D ** -0.5, 0.078125, ((0, 8),)),
        "query_states": draw_query_states(jax.random.fold_in(arg_keys[6], 71), 0),
        "key_states": draw_key_states(jax.random.fold_in(arg_keys[6], 71), 0),
        "cotangent": gaussian(arg_keys[4], (TOKENS, HEADS * HEAD_DIM), 1.0, 6.0, ((0, 32),)),
        "lengths": jax.vmap(lambda own: ragged_sizes(own, DOCS, PACK, MOST, 2))(jax.random.split(arg_keys[5], N_DP)).reshape((N_DP, DOCS)).astype(jnp.int32),
    }


def document_ids(lengths_row, positions):
    doc_ends = jnp.cumsum(lengths_row)
    return jnp.sum((positions[:, None] >= doc_ends[None, :-1]).astype(jnp.int32), axis=1)


def kv_group(operands):
    queries, keys_head, values_head, cot_head, lengths_row = operands
    positions = jnp.arange(PACK, dtype=jnp.int32)
    doc_ids = document_ids(lengths_row, positions)
    allowed = (doc_ids[:, None] == doc_ids[None, :]) & (positions[None, :] <= positions[:, None])
    score_scale = HEAD_DIM ** -0.5
    query_wide = queries.astype(jnp.float32)
    key_wide = keys_head.astype(jnp.float32)
    value_wide = values_head.astype(jnp.float32)
    cot_wide = cot_head.astype(jnp.float32)
    scores = jnp.einsum("qgd,kd->gqk", query_wide, key_wide) * score_scale
    scores = jnp.where(allowed[None], scores, -jnp.inf)
    highest = jnp.max(scores, axis=-1, keepdims=True)
    expo = jnp.exp(scores - highest)
    probabilities = expo / jnp.sum(expo, axis=-1, keepdims=True)
    rounded = lax.optimization_barrier(probabilities.astype(jnp.bfloat16)).astype(jnp.float32)
    attended = jnp.einsum("gqk,kd->qgd", rounded, value_wide).astype(jnp.bfloat16)
    attended = lax.optimization_barrier(attended)
    through_values = jnp.einsum("qgd,kd->gqk", cot_wide, value_wide)
    row_delta = jnp.einsum("qgd,qgd->gq", cot_wide, attended.astype(jnp.float32))
    score_grad = probabilities * (through_values - row_delta[:, :, None])
    score_grad = lax.optimization_barrier(score_grad.astype(jnp.bfloat16)).astype(jnp.float32)
    query_grad = (jnp.einsum("gqk,kd->qgd", score_grad, key_wide) * score_scale).astype(jnp.bfloat16)
    key_grad = (jnp.einsum("gqk,qgd->kd", score_grad, query_wide) * score_scale).astype(jnp.bfloat16)
    value_grad = jnp.einsum("gqk,qgd->kd", rounded, cot_wide).astype(jnp.bfloat16)
    return attended, query_grad, key_grad, value_grad


def reference(hidden_states, value_weight, query_states, key_states, cotangent, lengths):
    values = jnp.dot(hidden_states, value_weight, preferred_element_type=jnp.float32).astype(jnp.bfloat16)
    values = lax.optimization_barrier(values)
    group = HEADS // KV_HEADS

    def split_queries(table):
        shaped = table.reshape(N_DP, PACK, KV_HEADS, group, HEAD_DIM).transpose(0, 2, 1, 3, 4)
        return shaped.reshape(N_DP * KV_HEADS, PACK, group, HEAD_DIM)

    def split_keys(table):
        shaped = table.reshape(N_DP, PACK, KV_HEADS, HEAD_DIM).transpose(0, 2, 1, 3)
        return shaped.reshape(N_DP * KV_HEADS, PACK, HEAD_DIM)

    def join_queries(table):
        shaped = table.reshape(N_DP, KV_HEADS, PACK, group, HEAD_DIM).transpose(0, 2, 1, 3, 4)
        return shaped.reshape(TOKENS, HEADS * HEAD_DIM)

    def join_keys(table):
        shaped = table.reshape(N_DP, KV_HEADS, PACK, HEAD_DIM).transpose(0, 2, 1, 3)
        return shaped.reshape(TOKENS, KV_HEADS * HEAD_DIM)

    group_lengths = jnp.repeat(lengths, KV_HEADS, axis=0)
    attended, query_grad, key_grad, value_grad = lax.map(
        kv_group,
        (split_queries(query_states), split_keys(key_states), split_keys(values), split_queries(cotangent), group_lengths),
    )
    attention_out = join_queries(attended)
    query_out = join_queries(query_grad)
    key_out = join_keys(key_grad)
    value_rows = join_keys(value_grad)
    input_grad = jnp.dot(value_rows, value_weight.T, preferred_element_type=jnp.float32).astype(jnp.bfloat16)
    weight_grad = jnp.dot(hidden_states.T, value_rows, preferred_element_type=jnp.float32)
    return attention_out, query_out, key_out, input_grad, weight_grad
```

```python
import functools
import math

import jax
import jax.numpy as jnp
from jax import lax
from jax.experimental import pallas as pl
from jax.experimental.pallas import tpu as pltpu
from jax.sharding import PartitionSpec as P

HEADS = 64
KV_HEADS = 8
HEAD_DIM = 128
GROUP = HEADS // KV_HEADS
SCALE = HEAD_DIM ** (-0.5)
MESH = pl.DeviceIdType.MESH
BF = jnp.bfloat16
F32 = jnp.float32
PARTS = 4
AR_CUTS = 2

NT = (((1,), (1,)), ((), ()))


def mm(a, b, dims=(((1,), (0,)), ((), ()))):
    return lax.dot_general(a, b, dims, preferred_element_type=F32)


def kernel(
    n, seq, back, tok, depth, start_ref, hid, weight, query, keys, cot,
    out, dq, dk, ig, dw,
    hbuf, ht, wv, qv, cv, ov, dqv, kwin, vwin, pbuf, prec, csum, vrec,
    dpart, dsend, drec, dvall, igacc, igs, dwv, msg, rec_out, rec_in, tot,
    loc, hs, hr, ks, kr, ps, pr, vs, vr, vcs, vcr, ds_, dr, gs, gr, fs, fr, igss, igr,
    ais, air, aos, aor, osem, dwsem,
):
    chips = n // 2
    kv_cols = KV_HEADS * HEAD_DIM
    cols = kv_cols // PARTS
    heads_per = KV_HEADS // PARTS
    window = (back + 1) * tok
    d = lax.axis_index("dp")
    z = lax.axis_index("seq")
    c = lax.div(d, 2)
    k = lax.rem(d, 2)
    other = 1 - k
    partner = c * 2 + other
    pending = []

    def remote(src, dst, ssem, rsem, **where):
        return pltpu.make_async_remote_copy(
            src_ref=src, dst_ref=dst, send_sem=ssem, recv_sem=rsem,
            device_id=where, device_id_type=MESH,
        )

    def when(cond, fn):
        if cond is None:
            fn()
        else:
            pl.when(cond)(fn)

    def start(copy, cond=None):
        when(cond, lambda: copy.start())
        pending.append((cond, copy))

    kwin[pl.ds(0, back)] = jnp.zeros((back, tok, kv_cols), BF)
    vwin[:, pl.ds(0, back)] = jnp.zeros((PARTS, back, tok, cols), BF)

    barrier = pltpu.get_barrier_semaphore()
    for off in range(1, n):
        pl.semaphore_signal(barrier, 1, device_id={"dp": lax.rem(d + off, n)}, device_id_type=MESH)

    @pl.when(z > 0)
    def _():
        pl.semaphore_signal(barrier, 1, device_id={"seq": z - 1}, device_id_type=MESH)

    @pl.when(z < seq - 1)
    def _():
        pl.semaphore_signal(barrier, 1, device_id={"seq": z + 1}, device_id_type=MESH)

    def chunk(p):
        if depth % 128 == 0:
            return hid.at[:, pl.ds(pl.multiple_of(p * depth, 128), depth)]
        return hid.at[p]

    local = [
        pltpu.make_async_copy(chunk(d), hbuf.at[k, c], loc.at[0]),
        pltpu.make_async_copy(weight, wv, loc.at[1]),
        pltpu.make_async_copy(keys, kwin.at[back], loc.at[2]),
        pltpu.make_async_copy(query, qv, loc.at[3]),
        pltpu.make_async_copy(cot, cv, loc.at[4]),
    ]
    for copy in local:
        copy.start()
    inner = jnp.logical_and(z > 0, z < seq - 1)
    pl.semaphore_wait(barrier, n - 1 + jnp.where(inner, 2, 1))

    for off in range(n - 1, 0, -1):
        p = lax.rem(d + off, n)
        start(remote(chunk(p), hbuf.at[k, c], hs.at[off], hr.at[k, c], dp=p))

    def key_hop(s):
        src = keys if s == 1 else kwin.at[back - s + 1]
        cond = jnp.logical_and(z < seq - 1, z - s + 1 >= 0)
        start(remote(src, kwin.at[back - s], ks.at[s - 1], kr.at[s - 1], seq=z + 1), cond)

    def key_land(s):
        @pl.when(z - s >= 0)
        def _():
            remote(keys, kwin.at[back - s], ks.at[s - 1], kr.at[s - 1], seq=z).wait_recv()

    key_hop(1)
    local[0].wait()
    local[1].wait()

    def hidden_land(kk):
        for cc in range(chips):
            @pl.when(jnp.logical_or(cc != c, kk != k))
            def _():
                remote(hbuf.at[kk, cc], hbuf.at[kk, cc], hs.at[0], hr.at[kk, cc], dp=d).wait_recv()

    def partial_values(kk, gi):
        rows = hbuf[kk].reshape(chips * tok, depth)
        got = mm(rows, wv[:, gi * cols:(gi + 1) * cols])
        pbuf[gi, kk] = got.astype(BF).reshape(chips, tok, cols)

    hidden_land(other)
    for gi in range(PARTS):
        partial_values(other, gi)
        start(remote(pbuf.at[gi, other], prec.at[gi], ps.at[gi], pr.at[gi], dp=partner))
    hidden_land(k)
    for gi in range(PARTS):
        partial_values(k, gi)
    for gi in range(PARTS):
        remote(pbuf.at[gi, k], prec.at[gi], ps.at[gi], pr.at[gi], dp=partner).wait_recv()
        csum[gi] = (pbuf[gi, k].astype(F32) + prec[gi].astype(F32)).astype(BF)
        for co in range(1, chips):
            cc = lax.rem(c + co, chips)
            start(remote(
                csum.at[gi, cc], vrec.at[gi, c], vs.at[gi, co], vr.at[gi, c], dp=cc * 2 + k
            ))

    for s in range(2, back + 1):
        key_land(s - 1)
        key_hop(s)

    for kk in range(2):
        for cc in range(chips):
            ht[:, (kk * chips + cc) * tok:(kk * chips + cc + 1) * tok] = hbuf[kk, cc].T

    def value_hop(gi, s):
        cond = jnp.logical_and(z < seq - 1, z - s + 1 >= 0)
        start(remote(
            vwin.at[gi, back - s + 1], vwin.at[gi, back - s],
            vcs.at[gi, s - 1], vcr.at[gi, s - 1], seq=z + 1,
        ), cond)

    def value_land(gi, s):
        @pl.when(z - s >= 0)
        def _():
            remote(
                vwin.at[gi, back - s], vwin.at[gi, back - s],
                vcs.at[gi, s - 1], vcr.at[gi, s - 1], seq=z,
            ).wait_recv()

    def values_done(gi):
        total = csum[gi, c].astype(F32)
        for co in range(1, chips):
            cc = lax.rem(c + co, chips)
            remote(
                vrec.at[gi, cc], vrec.at[gi, cc], vs.at[gi, 0], vr.at[gi, cc], dp=d
            ).wait_recv()
            total += vrec[gi, cc].astype(F32)
        vwin[gi, back] = total.astype(BF)
        value_hop(gi, 1)

    def values_on(gi):
        for s in range(2, back + 1):
            value_land(gi, s - 1)
            value_hop(gi, s)

    def attention(gi):
        value_land(gi, back)
        key_at = (z - back) * tok + lax.broadcasted_iota(jnp.int32, (window, tok), 0)
        query_at = z * tok + lax.broadcasted_iota(jnp.int32, (window, tok), 1)
        first = start_ref[...]
        mask = jnp.logical_and(key_at >= first, key_at <= query_at)
        bias = jnp.where(mask, 0.0, -1e30).astype(F32)
        bias = jnp.concatenate([bias, bias], axis=1)

        def one(jl, carry):
            j = gi * heads_per + jl
            kcol = pl.ds(pl.multiple_of(j * HEAD_DIM, HEAD_DIM), HEAD_DIM)
            lcol = pl.ds(pl.multiple_of(jl * HEAD_DIM, HEAD_DIM), HEAD_DIM)
            kj = kwin[:, :, kcol].reshape(window, HEAD_DIM)
            vj = vwin[gi, :, :, lcol].reshape(window, HEAD_DIM)
            kt = kj.T
            vt = vj.T
            dkj = jnp.zeros((window, HEAD_DIM), F32)
            dvj = jnp.zeros((window, HEAD_DIM), F32)
            for pair in range(GROUP // 2):
                at = [
                    pl.ds(
                        pl.multiple_of((j * GROUP + pair * 2 + h) * HEAD_DIM, HEAD_DIM), HEAD_DIM
                    )
                    for h in range(2)
                ]
                qp = jnp.concatenate([qv[:, a] for a in at], axis=0)
                cp = jnp.concatenate([cv[:, a] for a in at], axis=0)
                st = mm(kj, qp, NT) * (SCALE * math.log2(math.e)) + bias
                dp = mm(vj, cp, NT)
                e = jnp.exp2(st - jnp.max(st, axis=0, keepdims=True))
                p = e * (1.0 / jnp.sum(e, axis=0, keepdims=True))
                pb = p.astype(BF)
                delta = jnp.sum(p * dp, axis=0, keepdims=True)
                sg = (p * (dp - delta)).astype(BF)
                dvj += mm(pb, cp)
                dkj += mm(sg, qp)
                ot = mm(vt, pb)
                qt = mm(kt, sg) * SCALE
                for h in range(2):
                    part = slice(h * HEAD_DIM, (h + 1) * HEAD_DIM)
                    ov[:, at[h]] = ot[:, part].T.astype(BF)
                    dqv[:, at[h]] = qt[:, part].T.astype(BF)
            dpart[0, gi, :, :, lcol] = dvj.reshape(back + 1, tok, HEAD_DIM)
            dpart[1, gi, :, :, lcol] = (dkj * SCALE).reshape(back + 1, tok, HEAD_DIM)
            return carry

        lax.fori_loop(0, heads_per, one, 0)
        wide = heads_per * GROUP * HEAD_DIM
        mine = pl.ds(gi * wide, wide)
        for index, (a, b) in enumerate(((ov, out), (dqv, dq))):
            copy = pltpu.make_async_copy(a.at[:, mine], b.at[:, mine], osem.at[gi, index])
            copy.start()
            pending.append((None, copy))

    def grad_copy(w, gi, i):
        return remote(
            dsend.at[w, gi, i], drec.at[w, gi, i], ds_.at[w, gi, i], dr.at[w, gi, i], seq=z - 1
        )

    def grad_step(w, gi, i):
        if i >= 1:
            @pl.when(jnp.logical_and(z < seq - 1, z - back + i >= 0))
            def _():
                grad_copy(w, gi, i - 1).wait_recv()
                dpart[w, gi, i] += drec[w, gi, i - 1].astype(F32)
        if i < back:
            dsend[w, gi, i] = dpart[w, gi, i].astype(BF)
            start(grad_copy(w, gi, i), z - back + i >= 0)

    def gather_send(gi):
        grad_step(0, gi, back)
        dvall[gi, k, c] = dpart[0, gi, back].astype(BF)
        for co in range(1, chips):
            cc = lax.rem(c + co, chips)
            start(remote(
                dvall.at[gi, k, c], dvall.at[gi, k, c], gs.at[gi, co], gr.at[gi, k, c], dp=cc * 2 + k
            ))
        start(remote(
            dvall.at[gi, k, c], dvall.at[gi, k, c], fs.at[gi, 0], gr.at[gi, k, c], dp=partner
        ))
        grad_step(1, gi, back)
        dk[:, gi * cols:(gi + 1) * cols] = dpart[1, gi, back].astype(BF)

    def gather_land(gi, kk, cc):
        remote(
            dvall.at[gi, kk, cc], dvall.at[gi, kk, cc], gs.at[gi, 0], gr.at[gi, kk, cc], dp=d
        ).wait_recv()

    def gather_on(gi):
        for co in range(1, chips):
            cc = lax.rem(c + co, chips)
            gather_land(gi, k, cc)
            start(remote(
                dvall.at[gi, k, cc], dvall.at[gi, k, cc], fs.at[gi, co], gr.at[gi, k, cc], dp=partner
            ))

    half = seq // 2
    low = z < half
    inward = jnp.where(low, z + 1, z - 1)
    outward = jnp.where(low, z - 1, z + 1)
    middle = jnp.logical_or(z == half - 1, z == half)
    edge = jnp.logical_or(z == 0, z == seq - 1)
    not_middle = jnp.logical_not(middle)
    not_edge = jnp.logical_not(edge)
    cut = depth // AR_CUTS

    def weight_grad(gi):
        for cc in range(chips):
            gather_land(gi, other, cc)
        rows = dvall[gi].reshape(n * tok, cols)
        dwv[gi] = mm(ht[...], rows)
        for r in range(AR_CUTS):
            reduce_in(gi, r, True)

    def reduce_in(gi, r, first):
        at = (gi, pl.ds(r * cut, cut))

        def send():
            msg[at] = dwv[at].astype(BF)

        if first:
            @pl.when(edge)
            def _():
                send()
            cond = edge
        else:
            @pl.when(not_edge)
            def _():
                remote(msg.at[at], rec_out.at[at], ais.at[gi, r], aor.at[gi, r], seq=z).wait_recv()
                dwv[at] += rec_out[at].astype(F32)
                send()
            cond = not_edge
        a = jnp.logical_and(cond, not_middle)
        b = jnp.logical_and(cond, middle)
        start(remote(msg.at[at], rec_out.at[at], ais.at[gi, r], aor.at[gi, r], seq=inward), a)
        start(remote(msg.at[at], rec_in.at[at], ais.at[gi, r], air.at[gi, r], seq=inward), b)

    def reduce_out(gi, r):
        at = (gi, pl.ds(r * cut, cut))
        remote(msg.at[at], rec_in.at[at], ais.at[gi, r], air.at[gi, r], seq=z).wait_recv()

        @pl.when(middle)
        def _():
            tot[at] = (msg[at].astype(F32) + rec_in[at].astype(F32)).astype(BF)

        @pl.when(not_middle)
        def _():
            tot[at] = rec_in[at]

        start(remote(tot.at[at], rec_in.at[at], aos.at[gi, r], air.at[gi, r], seq=outward), not_edge)
        dwv[at] = tot[at].astype(F32)
        copy = pltpu.make_async_copy(
            dwv.at[at], dw.at[pl.ds(r * cut, cut), pl.ds(gi * cols, cols)], dwsem.at[gi, r]
        )
        copy.start()
        pending.append((None, copy))

    def input_grad(gi):
        rows = dvall[gi].reshape(n * tok, cols)
        got = mm(rows, wv[:, gi * cols:(gi + 1) * cols], NT)
        if gi == 0:
            igacc[...] = got
        elif gi < PARTS - 1:
            igacc[...] += got
        else:
            igs[...] = (igacc[...] + got).astype(BF).reshape(2, chips, tok, depth)
            for off in range(1, n):
                p = lax.rem(d + off, n)
                start(remote(
                    igs.at[lax.rem(p, 2), lax.div(p, 2)], ig.at[k, c],
                    igss.at[off], igr.at[k, c], dp=p,
                ))
            copy = pltpu.make_async_copy(igs.at[k, c], ig.at[k, c], loc.at[5])
            copy.start()
            pending.append((None, copy))

    for gi in range(PARTS):
        values_done(gi)
    local[2].wait()
    local[3].wait()
    local[4].wait()
    key_land(back)

    def grads_start(gi):
        attention(gi)
        grad_step(0, gi, 0)
        grad_step(1, gi, 0)

    def grads_on(gi):
        for i in range(1, back):
            grad_step(0, gi, i)
            grad_step(1, gi, i)

    def reduces(gi):
        for r in range(AR_CUTS):
            reduce_in(gi, r, False)

    def finish(gi):
        for r in range(AR_CUTS):
            reduce_out(gi, r)

    stages = [values_on, grads_start, grads_on, gather_send, gather_on, weight_grad, input_grad, reduces, finish]
    for t in range(PARTS + len(stages) - 1):
        for s in range(len(stages)):
            if 0 <= t - s < PARTS:
                stages[s](t - s)

    for off in range(1, n):
        p = lax.rem(d + off, n)
        slot = (lax.rem(p, 2), lax.div(p, 2))
        remote(igs.at[slot], ig.at[slot], igss.at[0], igr.at[slot], dp=d).wait_recv()
    for cond, copy in pending:
        if hasattr(copy, "wait_send") and copy.is_remote:
            when(cond, lambda copy=copy: copy.wait_send())
        else:
            copy.wait()


def body(hidden_states, value_weight, query_states, key_states, cotangent, lengths, n, seq):
    tok, width = hidden_states.shape
    depth = value_weight.shape[0]
    kv_cols = value_weight.shape[1]
    cols = kv_cols // PARTS
    chips = n // 2
    packed = tok * seq
    back = -(-(packed // 2 - 1) // tok)
    ends = jnp.cumsum(lengths[0])[:-1]
    at = lax.axis_index("seq") * tok + jnp.arange(tok, dtype=jnp.int32)
    first = jnp.max(jnp.where(ends[:, None] <= at[None, :], ends[:, None], 0), axis=0)[None, :]
    hid = hidden_states
    if depth % 128:
        hid = hid.reshape(tok, n, depth).transpose(1, 0, 2)
    vmem = pl.BlockSpec(memory_space=pltpu.VMEM)
    hbm = pl.BlockSpec(memory_space=pl.ANY)
    dma = pltpu.SemaphoreType.DMA
    out, dq, dk, ig, dw = pl.pallas_call(
        functools.partial(kernel, n, seq, back, tok, depth),
        out_shape=(
            jax.ShapeDtypeStruct(query_states.shape, BF),
            jax.ShapeDtypeStruct(query_states.shape, BF),
            jax.ShapeDtypeStruct(key_states.shape, BF),
            jax.ShapeDtypeStruct((2, chips, tok, depth), BF),
            jax.ShapeDtypeStruct((depth, kv_cols), F32),
        ),
        in_specs=[vmem, hbm, hbm, hbm, hbm, hbm],
        out_specs=(hbm, hbm, vmem, hbm, hbm),
        scratch_shapes=[
            pltpu.VMEM((2, chips, tok, depth), BF),
            pltpu.VMEM((depth, n * tok), BF),
            pltpu.VMEM((depth, kv_cols), BF),
            pltpu.VMEM(query_states.shape, BF),
            pltpu.VMEM(query_states.shape, BF),
            pltpu.VMEM(query_states.shape, BF),
            pltpu.VMEM(query_states.shape, BF),
            pltpu.VMEM((back + 1, tok, kv_cols), BF),
            pltpu.VMEM((PARTS, back + 1, tok, cols), BF),
            pltpu.VMEM((PARTS, 2, chips, tok, cols), BF),
            pltpu.VMEM((PARTS, chips, tok, cols), BF),
            pltpu.VMEM((PARTS, chips, tok, cols), BF),
            pltpu.VMEM((PARTS, chips, tok, cols), BF),
            pltpu.VMEM((2, PARTS, back + 1, tok, cols), F32),
            pltpu.VMEM((2, PARTS, back, tok, cols), BF),
            pltpu.VMEM((2, PARTS, back, tok, cols), BF),
            pltpu.VMEM((PARTS, 2, chips, tok, cols), BF),
            pltpu.VMEM((n * tok, depth), F32),
            pltpu.VMEM((2, chips, tok, depth), BF),
            pltpu.VMEM((PARTS, depth, cols), F32),
            pltpu.VMEM((PARTS, depth, cols), BF),
            pltpu.VMEM((PARTS, depth, cols), BF),
            pltpu.VMEM((PARTS, depth, cols), BF),
            pltpu.VMEM((PARTS, depth, cols), BF),
            dma((6,)),
            dma((n,)), dma((2, chips)),
            dma((back,)), dma((back,)),
            dma((PARTS,)), dma((PARTS,)),
            dma((PARTS, chips)), dma((PARTS, chips)),
            dma((PARTS, back)), dma((PARTS, back)),
            dma((2, PARTS, back)), dma((2, PARTS, back)),
            dma((PARTS, chips)), dma((PARTS, 2, chips)),
            dma((PARTS, chips)), dma((1,)),
            dma((n,)), dma((2, chips)),
            dma((PARTS, AR_CUTS)), dma((PARTS, AR_CUTS)),
            dma((PARTS, AR_CUTS)), dma((PARTS, AR_CUTS)),
            dma((PARTS, 2)), dma((PARTS, AR_CUTS)),
        ],
        compiler_params=pltpu.CompilerParams(
            collective_id=0, has_side_effects=True, vmem_limit_bytes=60 * 1024 * 1024
        ),
    )(first, hid, value_weight, query_states, key_states, cotangent)
    input_grad = ig.transpose(2, 1, 0, 3).reshape(tok, width)
    return out, dq, dk, input_grad, dw


def solution(mesh):
    rows = P(("dp", "seq"), None)
    placed = (rows, P("dp", None), rows, rows, rows, P("dp", None))
    return jax.shard_map(
        functools.partial(body, n=mesh.shape["dp"], seq=mesh.shape["seq"]),
        mesh=mesh,
        in_specs=placed,
        out_specs=(rows, rows, rows, rows, P("dp", None)),
        check_vma=False,
    )
```

```python
import functools
import math

import jax
import jax.numpy as jnp
from jax import lax
from jax.experimental import pallas as pl
from jax.experimental.pallas import tpu as pltpu
from jax.sharding import PartitionSpec as P

HEADS = 64
KV_HEADS = 8
HEAD_DIM = 128
GROUP = HEADS // KV_HEADS
SCALE = HEAD_DIM ** (-0.5)
MESH = pl.DeviceIdType.MESH
BF = jnp.bfloat16
F32 = jnp.float32
PARTS = 4
AR_CUTS = 2

NT = (((1,), (1,)), ((), ()))


def mm(a, b, dims=(((1,), (0,)), ((), ()))):
    return lax.dot_general(a, b, dims, preferred_element_type=F32)


def kernel(
    n, seq, back, tok, depth, lengths, hid, weight, query, keys, cot,
    out, dq, dk, ig, dw,
    hbuf, ht, wv, qv, cv, ov, dqv, kwin, vwin, probs, pbuf, prec, csum, vrec,
    dpart, dsend, drec, dvall, igacc, igs, dwv, msg, rec_out, rec_in, tot,
    loc, hs, hr, ks, kr, ps, pr, vs, vr, vcs, vcr, ds_, dr, gs, gr, fs, fr, igss, igr,
    ais, air, aos, aor, osem, dwsem,
):
    chips = n // 2
    kv_cols = KV_HEADS * HEAD_DIM
    cols = kv_cols // PARTS
    heads_per = KV_HEADS // PARTS
    window = (back + 1) * tok
    d = lax.axis_index("dp")
    z = lax.axis_index("seq")
    c = lax.div(d, 2)
    k = lax.rem(d, 2)
    other = 1 - k
    partner = c * 2 + other
    pending = []

    def remote(src, dst, ssem, rsem, **where):
        return pltpu.make_async_remote_copy(
            src_ref=src, dst_ref=dst, send_sem=ssem, recv_sem=rsem,
            device_id=where, device_id_type=MESH,
        )

    def when(cond, fn):
        if cond is None:
            fn()
        else:
            pl.when(cond)(fn)

    def start(copy, cond=None):
        when(cond, lambda: copy.start())
        pending.append((cond, copy))

    kwin[:, pl.ds(0, back)] = jnp.zeros((PARTS, back, tok, cols), BF)
    vwin[:, pl.ds(0, back)] = jnp.zeros((PARTS, back, tok, cols), BF)

    barrier = pltpu.get_barrier_semaphore()
    for off in range(1, n):
        pl.semaphore_signal(barrier, 1, device_id={"dp": lax.rem(d + off, n)}, device_id_type=MESH)

    @pl.when(z > 0)
    def _():
        pl.semaphore_signal(barrier, 1, device_id={"seq": z - 1}, device_id_type=MESH)

    @pl.when(z < seq - 1)
    def _():
        pl.semaphore_signal(barrier, 1, device_id={"seq": z + 1}, device_id_type=MESH)

    def chunk(p):
        if depth % 128 == 0:
            return hid.at[:, pl.ds(pl.multiple_of(p * depth, 128), depth)]
        return hid.at[p]

    local = [
        pltpu.make_async_copy(chunk(d), hbuf.at[k, c], loc.at[0]),
        pltpu.make_async_copy(weight, wv, loc.at[1]),
        pltpu.make_async_copy(query, qv, loc.at[2]),
        pltpu.make_async_copy(cot, cv, loc.at[3]),
    ] + [
        pltpu.make_async_copy(keys.at[:, pl.ds(gi * cols, cols)], kwin.at[gi, back], loc.at[5 + gi])
        for gi in range(PARTS)
    ]
    for copy in local:
        copy.start()
    inner = jnp.logical_and(z > 0, z < seq - 1)
    pl.semaphore_wait(barrier, n - 1 + jnp.where(inner, 2, 1))

    def key_hop(gi, s):
        src = keys.at[:, pl.ds(gi * cols, cols)] if s == 1 else kwin.at[gi, back - s + 1]
        cond = jnp.logical_and(z < seq - 1, z - s + 1 >= 0)
        start(remote(
            src, kwin.at[gi, back - s], ks.at[gi, s - 1], kr.at[gi, s - 1], seq=z + 1
        ), cond)

    def key_land(gi, s):
        @pl.when(z - s >= 0)
        def _():
            remote(
                kwin.at[gi, back - s], kwin.at[gi, back - s],
                ks.at[gi, s - 1], kr.at[gi, s - 1], seq=z,
            ).wait_recv()

    def keys_on(gi):
        for s in range(2, back + 1):
            key_land(gi, s - 1)
            key_hop(gi, s)

    for gi in range(PARTS):
        key_hop(gi, 1)
    for off in range(n - 1, 0, -1):
        p = lax.rem(d + off, n)
        start(remote(chunk(p), hbuf.at[k, c], hs.at[off], hr.at[k, c], dp=p))

    def hidden_land(kk):
        for cc in range(chips):
            @pl.when(jnp.logical_or(cc != c, kk != k))
            def _():
                remote(hbuf.at[kk, cc], hbuf.at[kk, cc], hs.at[0], hr.at[kk, cc], dp=d).wait_recv()

    def partial_values(kk, gi):
        rows = hbuf[kk].reshape(chips * tok, depth)
        got = mm(rows, wv[:, gi * cols:(gi + 1) * cols])
        pbuf[gi, kk] = got.astype(BF).reshape(chips, tok, cols)

    def values_pair():
        local[0].wait()
        local[1].wait()
        hidden_land(other)
        for gi in range(PARTS):
            partial_values(other, gi)
            start(remote(pbuf.at[gi, other], prec.at[gi], ps.at[gi], pr.at[gi], dp=partner))

    def values_own():
        hidden_land(k)
        for gi in range(PARTS):
            partial_values(k, gi)

    def values_send(gi):
        remote(pbuf.at[gi, k], prec.at[gi], ps.at[gi], pr.at[gi], dp=partner).wait_recv()
        csum[gi] = (pbuf[gi, k].astype(F32) + prec[gi].astype(F32)).astype(BF)
        for co in range(1, chips):
            cc = lax.rem(c + co, chips)
            start(remote(
                csum.at[gi, cc], vrec.at[gi, c], vs.at[gi, co], vr.at[gi, c], dp=cc * 2 + k
            ))

    def turn_hidden():
        for kk in range(2):
            for cc in range(chips):
                ht[:, (kk * chips + cc) * tok:(kk * chips + cc + 1) * tok] = hbuf[kk, cc].T

    def value_hop(gi, s):
        cond = jnp.logical_and(z < seq - 1, z - s + 1 >= 0)
        start(remote(
            vwin.at[gi, back - s + 1], vwin.at[gi, back - s],
            vcs.at[gi, s - 1], vcr.at[gi, s - 1], seq=z + 1,
        ), cond)

    def value_land(gi, s):
        @pl.when(z - s >= 0)
        def _():
            remote(
                vwin.at[gi, back - s], vwin.at[gi, back - s],
                vcs.at[gi, s - 1], vcr.at[gi, s - 1], seq=z,
            ).wait_recv()

    def values_done(gi):
        total = csum[gi, c].astype(F32)
        for co in range(1, chips):
            cc = lax.rem(c + co, chips)
            remote(
                vrec.at[gi, cc], vrec.at[gi, cc], vs.at[gi, 0], vr.at[gi, cc], dp=d
            ).wait_recv()
            total += vrec[gi, cc].astype(F32)
        vwin[gi, back] = total.astype(BF)
        value_hop(gi, 1)

    def values_on(gi):
        for s in range(2, back + 1):
            value_land(gi, s - 1)
            value_hop(gi, s)

    def pair_rows(j, pair):
        at = [slice((j * GROUP + pair * 2 + h) * HEAD_DIM, (j * GROUP + pair * 2 + h + 1) * HEAD_DIM)
              for h in range(2)]
        qp = jnp.concatenate([qv[:, a] for a in at], axis=0)
        cp = jnp.concatenate([cv[:, a] for a in at], axis=0)
        return at, qp, cp

    def scores(gi):
        local[5 + gi - 1].wait()
        key_land(gi, back)
        key_at = (z - back) * tok + lax.broadcasted_iota(jnp.int32, (window, tok), 0)
        query_at = z * tok + lax.broadcasted_iota(jnp.int32, (window, tok), 1)
        own_at = z * tok + lax.broadcasted_iota(jnp.int32, (1, tok), 1)
        first = jnp.zeros((1, tok), jnp.int32)
        end = 0
        for r in range(lengths.shape[1] - 1):
            end = end + lengths[0, r]
            first = jnp.where(own_at >= end, end, first)
        mask = jnp.logical_and(key_at >= first, key_at <= query_at)
        bias = jnp.where(mask, 0.0, -1e30).astype(F32)
        bias = jnp.concatenate([bias, bias], axis=1)
        for jl in range(heads_per):
            j = gi * heads_per + jl
            lcol = slice(jl * HEAD_DIM, (jl + 1) * HEAD_DIM)
            kj = kwin[gi, :, :, lcol].reshape(window, HEAD_DIM)
            dvj = jnp.zeros((window, HEAD_DIM), F32)
            for pair in range(GROUP // 2):
                at, qp, cp = pair_rows(j, pair)
                st = mm(kj, qp, NT) * (SCALE * math.log2(math.e)) + bias
                e = jnp.exp2(st - jnp.max(st, axis=0, keepdims=True))
                pb = (e * (1.0 / jnp.sum(e, axis=0, keepdims=True))).astype(BF)
                probs[j, pair] = pb
                dvj += mm(pb, cp)
            dpart[0, gi, :, :, lcol] = dvj.reshape(back + 1, tok, HEAD_DIM)
        grad_step(0, gi, 0)

    def through(j):
        gi, jl = divmod(j, heads_per)
        if jl == 0:
            value_land(gi, back)
        lcol = slice(jl * HEAD_DIM, (jl + 1) * HEAD_DIM)
        kt = kwin[gi, :, :, lcol].reshape(window, HEAD_DIM).T
        vj = vwin[gi, :, :, lcol].reshape(window, HEAD_DIM)
        vt = vj.T
        dkj = jnp.zeros((window, HEAD_DIM), F32)
        for pair in range(GROUP // 2):
            at, qp, cp = pair_rows(j, pair)
            pb = probs[j, pair]
            p = pb.astype(F32)
            dp = mm(vj, cp, NT)
            delta = jnp.sum(p * dp, axis=0, keepdims=True)
            sg = (p * (dp - delta)).astype(BF)
            dkj += mm(sg, qp)
            ot = mm(vt, pb)
            qt = mm(kt, sg) * SCALE
            for h in range(2):
                part = slice(h * HEAD_DIM, (h + 1) * HEAD_DIM)
                ov[:, at[h]] = ot[:, part].T.astype(BF)
                dqv[:, at[h]] = qt[:, part].T.astype(BF)
        dpart[1, gi, :, :, lcol] = (dkj * SCALE).reshape(back + 1, tok, HEAD_DIM)
        if jl == heads_per - 1:
            grad_step(1, gi, 0)
            wide = heads_per * GROUP * HEAD_DIM
            mine = pl.ds(gi * wide, wide)
            for index, (a, b) in enumerate(((ov, out), (dqv, dq))):
                copy = pltpu.make_async_copy(a.at[:, mine], b.at[:, mine], osem.at[gi, index])
                copy.start()
                pending.append((None, copy))

    def grad_copy(w, gi, i):
        return remote(
            dsend.at[w, gi, i], drec.at[w, gi, i], ds_.at[w, gi, i], dr.at[w, gi, i], seq=z - 1
        )

    def grad_step(w, gi, i):
        if i >= 1:
            @pl.when(jnp.logical_and(z < seq - 1, z - back + i >= 0))
            def _():
                grad_copy(w, gi, i - 1).wait_recv()
                dpart[w, gi, i] += drec[w, gi, i - 1].astype(F32)
        if i < back:
            dsend[w, gi, i] = dpart[w, gi, i].astype(BF)
            start(grad_copy(w, gi, i), z - back + i >= 0)

    def gather_send(gi):
        grad_step(0, gi, back)
        dvall[gi, k, c] = dpart[0, gi, back].astype(BF)
        for co in range(1, chips):
            cc = lax.rem(c + co, chips)
            start(remote(
                dvall.at[gi, k, c], dvall.at[gi, k, c], gs.at[gi, co], gr.at[gi, k, c], dp=cc * 2 + k
            ))
        start(remote(
            dvall.at[gi, k, c], dvall.at[gi, k, c], fs.at[gi, 0], gr.at[gi, k, c], dp=partner
        ))

    def key_grads(gi):
        grad_step(1, gi, back)
        dk[:, gi * cols:(gi + 1) * cols] = dpart[1, gi, back].astype(BF)

    def gather_land(gi, kk, cc):
        remote(
            dvall.at[gi, kk, cc], dvall.at[gi, kk, cc], gs.at[gi, 0], gr.at[gi, kk, cc], dp=d
        ).wait_recv()

    def gather_on(gi):
        for co in range(1, chips):
            cc = lax.rem(c + co, chips)
            gather_land(gi, k, cc)
            start(remote(
                dvall.at[gi, k, cc], dvall.at[gi, k, cc], fs.at[gi, co], gr.at[gi, k, cc], dp=partner
            ))

    half = seq // 2
    low = z < half
    inward = jnp.where(low, z + 1, z - 1)
    outward = jnp.where(low, z - 1, z + 1)
    middle = jnp.logical_or(z == half - 1, z == half)
    edge = jnp.logical_or(z == 0, z == seq - 1)
    not_middle = jnp.logical_not(middle)
    not_edge = jnp.logical_not(edge)
    cut = depth // AR_CUTS

    def weight_grad(gi):
        for cc in range(chips):
            gather_land(gi, other, cc)
        rows = dvall[gi].reshape(n * tok, cols)
        dwv[gi] = mm(ht[...], rows)
        for r in range(AR_CUTS):
            reduce_in(gi, r, True)

    def reduce_in(gi, r, first):
        at = (gi, pl.ds(r * cut, cut))

        def send():
            msg[at] = dwv[at].astype(BF)

        if first:
            @pl.when(edge)
            def _():
                send()
            cond = edge
        else:
            @pl.when(not_edge)
            def _():
                remote(msg.at[at], rec_out.at[at], ais.at[gi, r], aor.at[gi, r], seq=z).wait_recv()
                dwv[at] += rec_out[at].astype(F32)
                send()
            cond = not_edge
        a = jnp.logical_and(cond, not_middle)
        b = jnp.logical_and(cond, middle)
        start(remote(msg.at[at], rec_out.at[at], ais.at[gi, r], aor.at[gi, r], seq=inward), a)
        start(remote(msg.at[at], rec_in.at[at], ais.at[gi, r], air.at[gi, r], seq=inward), b)

    def reduce_out(gi, r):
        at = (gi, pl.ds(r * cut, cut))
        remote(msg.at[at], rec_in.at[at], ais.at[gi, r], air.at[gi, r], seq=z).wait_recv()

        @pl.when(middle)
        def _():
            tot[at] = (msg[at].astype(F32) + rec_in[at].astype(F32)).astype(BF)

        @pl.when(not_middle)
        def _():
            tot[at] = rec_in[at]

        start(remote(tot.at[at], rec_in.at[at], aos.at[gi, r], air.at[gi, r], seq=outward), not_edge)
        dwv[at] = tot[at].astype(F32)
        copy = pltpu.make_async_copy(
            dwv.at[at], dw.at[pl.ds(r * cut, cut), pl.ds(gi * cols, cols)], dwsem.at[gi, r]
        )
        copy.start()
        pending.append((None, copy))

    def block(p):
        if depth % 128 == 0:
            return ig.at[:, pl.ds(pl.multiple_of(p * depth, 128), depth)]
        return ig.at[p]

    def input_grad(gi):
        rows = dvall[gi].reshape(n * tok, cols)
        got = mm(rows, wv[:, gi * cols:(gi + 1) * cols], NT)
        if gi == 0:
            igacc[...] = got
        elif gi < PARTS - 1:
            igacc[...] += got
        else:
            igs[...] = (igacc[...] + got).astype(BF).reshape(2, chips, tok, depth)
            for off in range(1, n):
                p = lax.rem(d + off, n)
                start(remote(
                    igs.at[lax.rem(p, 2), lax.div(p, 2)], block(d),
                    igss.at[off], igr.at[k, c], dp=p,
                ))
            copy = pltpu.make_async_copy(igs.at[k, c], block(d), loc.at[4])
            copy.start()
            pending.append((None, copy))

    def grads_on(w, gi):
        for i in range(1, back):
            grad_step(w, gi, i)

    def value_grads_on(gi):
        grads_on(0, gi)

    def key_grads_on(gi):
        grads_on(1, gi)

    def reduces(gi):
        for r in range(AR_CUTS):
            reduce_in(gi, r, False)

    def finish(gi):
        for r in range(AR_CUTS):
            reduce_out(gi, r)

    def later(*rows):
        for row in rows:
            for at in range(0, len(row), 2):
                row[at](row[at + 1])

    local[2].wait()
    local[3].wait()
    later(
        (keys_on, 0, keys_on, 1, keys_on, 2),
        (scores, 0, keys_on, 3),
        (scores, 1, value_grads_on, 0),
        (scores, 2, value_grads_on, 1, gather_send, 0),
        (scores, 3, value_grads_on, 2, gather_send, 1),
    )
    values_pair()
    later((value_grads_on, 3, gather_send, 2))
    values_own()
    later((gather_send, 3))
    for gi in range(PARTS):
        values_send(gi)
    turn_hidden()
    later(
        (gather_on, 0, gather_on, 1, weight_grad, 0),
        (gather_on, 2, weight_grad, 1, reduces, 0),
        (gather_on, 3, weight_grad, 2, reduces, 1, finish, 0),
        (values_done, 0, weight_grad, 3, reduces, 2, finish, 1),
        (values_done, 1, values_on, 0, reduces, 3),
        (values_done, 2, values_on, 1),
        (values_done, 3, values_on, 2),
        (input_grad, 0, input_grad, 1, input_grad, 2, input_grad, 3),
        (through, 0, values_on, 3, finish, 2),
        (through, 1, through, 2, finish, 3, key_grads_on, 0),
        (through, 3, through, 4, key_grads_on, 1, key_grads, 0),
        (through, 5, through, 6, key_grads_on, 2, key_grads, 1),
        (through, 7, key_grads, 2, key_grads_on, 3, key_grads, 3),
    )

    for off in range(1, n):
        p = lax.rem(d + off, n)
        slot = (lax.rem(p, 2), lax.div(p, 2))
        remote(igs.at[slot], block(p), igss.at[0], igr.at[slot], dp=d).wait_recv()
    for cond, copy in pending:
        if hasattr(copy, "wait_send") and copy.is_remote:
            when(cond, lambda copy=copy: copy.wait_send())
        else:
            copy.wait()


def body(hidden_states, value_weight, query_states, key_states, cotangent, lengths, n, seq):
    tok, width = hidden_states.shape
    depth = value_weight.shape[0]
    kv_cols = value_weight.shape[1]
    cols = kv_cols // PARTS
    chips = n // 2
    packed = tok * seq
    back = -(-(packed // 2 - 1) // tok)
    hid = hidden_states
    aligned = depth % 128 == 0
    if not aligned:
        hid = hid.reshape(tok, n, depth).transpose(1, 0, 2)
    vmem = pl.BlockSpec(memory_space=pltpu.VMEM)
    hbm = pl.BlockSpec(memory_space=pl.ANY)
    dma = pltpu.SemaphoreType.DMA
    out, dq, dk, ig, dw = pl.pallas_call(
        functools.partial(kernel, n, seq, back, tok, depth),
        out_shape=(
            jax.ShapeDtypeStruct(query_states.shape, BF),
            jax.ShapeDtypeStruct(query_states.shape, BF),
            jax.ShapeDtypeStruct(key_states.shape, BF),
            jax.ShapeDtypeStruct((tok, width) if aligned else (n, tok, depth), BF),
            jax.ShapeDtypeStruct((depth, kv_cols), F32),
        ),
        in_specs=[pl.BlockSpec(memory_space=pltpu.SMEM), hbm, hbm, hbm, hbm, hbm],
        out_specs=(hbm, hbm, vmem, hbm, hbm),
        scratch_shapes=[
            pltpu.VMEM((2, chips, tok, depth), BF),
            pltpu.VMEM((depth, n * tok), BF),
            pltpu.VMEM((depth, kv_cols), BF),
            pltpu.VMEM(query_states.shape, BF),
            pltpu.VMEM(query_states.shape, BF),
            pltpu.VMEM(query_states.shape, BF),
            pltpu.VMEM(query_states.shape, BF),
            pltpu.VMEM((PARTS, back + 1, tok, cols), BF),
            pltpu.VMEM((PARTS, back + 1, tok, cols), BF),
            pltpu.VMEM((KV_HEADS, GROUP // 2, (back + 1) * tok, 2 * tok), BF),
            pltpu.VMEM((PARTS, 2, chips, tok, cols), BF),
            pltpu.VMEM((PARTS, chips, tok, cols), BF),
            pltpu.VMEM((PARTS, chips, tok, cols), BF),
            pltpu.VMEM((PARTS, chips, tok, cols), BF),
            pltpu.VMEM((2, PARTS, back + 1, tok, cols), F32),
            pltpu.VMEM((2, PARTS, back, tok, cols), BF),
            pltpu.VMEM((2, PARTS, back, tok, cols), BF),
            pltpu.VMEM((PARTS, 2, chips, tok, cols), BF),
            pltpu.VMEM((n * tok, depth), F32),
            pltpu.VMEM((2, chips, tok, depth), BF),
            pltpu.VMEM((PARTS, depth, cols), F32),
            pltpu.VMEM((PARTS, depth, cols), BF),
            pltpu.VMEM((PARTS, depth, cols), BF),
            pltpu.VMEM((PARTS, depth, cols), BF),
            pltpu.VMEM((PARTS, depth, cols), BF),
            dma((5 + PARTS,)),
            dma((n,)), dma((2, chips)),
            dma((PARTS, back)), dma((PARTS, back)),
            dma((PARTS,)), dma((PARTS,)),
            dma((PARTS, chips)), dma((PARTS, chips)),
            dma((PARTS, back)), dma((PARTS, back)),
            dma((2, PARTS, back)), dma((2, PARTS, back)),
            dma((PARTS, chips)), dma((PARTS, 2, chips)),
            dma((PARTS, chips)), dma((1,)),
            dma((n,)), dma((2, chips)),
            dma((PARTS, AR_CUTS)), dma((PARTS, AR_CUTS)),
            dma((PARTS, AR_CUTS)), dma((PARTS, AR_CUTS)),
            dma((PARTS, 2)), dma((PARTS, AR_CUTS)),
        ],
        compiler_params=pltpu.CompilerParams(
            collective_id=0, has_side_effects=True, vmem_limit_bytes=60 * 1024 * 1024
        ),
    )(lengths, hid, value_weight, query_states, key_states, cotangent)
    if not aligned:
        ig = ig.transpose(1, 0, 2).reshape(tok, width)
    return out, dq, dk, ig, dw


def solution(mesh):
    rows = P(("dp", "seq"), None)
    placed = (rows, P("dp", None), rows, rows, rows, P("dp", None))
    return jax.shard_map(
        functools.partial(body, n=mesh.shape["dp"], seq=mesh.shape["seq"]),
        mesh=mesh,
        in_specs=placed,
        out_specs=(rows, rows, rows, rows, P("dp", None)),
        check_vma=False,
    )
```

```python
import functools
import math

import jax
import jax.numpy as jnp
from jax import lax
from jax.experimental import pallas as pl
from jax.experimental.pallas import tpu as pltpu
from jax.sharding import PartitionSpec as P

HEADS = 64
KV_HEADS = 8
HEAD_DIM = 128
GROUP = HEADS // KV_HEADS
SCALE = HEAD_DIM ** (-0.5)
MESH = pl.DeviceIdType.MESH
BF = jnp.bfloat16
F32 = jnp.float32
PARTS = 4
AR_CUTS = 2

NT = (((1,), (1,)), ((), ()))


def mm(a, b, dims=(((1,), (0,)), ((), ()))):
    return lax.dot_general(a, b, dims, preferred_element_type=F32)


def kernel(
    n, seq, back, tok, depth, lengths, hid, weight, query, keys, cot,
    out, dq, dk, ig, dw,
    hbuf, ht, wv, qv, cv, ov, dqv, kwin, vwin, probs, pbuf, prec, csum, vrec,
    dpart, dsend, drec, dvall, igacc, igs, dwv, msg, rec_out, rec_in, tot,
    loc, hs, hr, ks, kr, ps, pr, vs, vr, vcs, vcr, ds_, dr, gs, gr, fs, fr, igss, igr,
    ais, air, aos, aor, osem, dwsem,
):
    chips = n // 2
    kv_cols = KV_HEADS * HEAD_DIM
    cols = kv_cols // PARTS
    heads_per = KV_HEADS // PARTS
    window = (back + 1) * tok
    d = lax.axis_index("dp")
    z = lax.axis_index("seq")
    c = lax.div(d, 2)
    k = lax.rem(d, 2)
    other = 1 - k
    partner = c * 2 + other
    pending = []

    def remote(src, dst, ssem, rsem, **where):
        return pltpu.make_async_remote_copy(
            src_ref=src, dst_ref=dst, send_sem=ssem, recv_sem=rsem,
            device_id=where, device_id_type=MESH,
        )

    def when(cond, fn):
        if cond is None:
            fn()
        else:
            pl.when(cond)(fn)

    def start(copy, cond=None):
        when(cond, lambda: copy.start())
        pending.append((cond, copy))

    kwin[:, pl.ds(0, back)] = jnp.zeros((PARTS, back, tok, cols), BF)
    vwin[:, pl.ds(0, back)] = jnp.zeros((PARTS, back, tok, cols), BF)

    barrier = pltpu.get_barrier_semaphore()
    for off in range(1, n):
        pl.semaphore_signal(barrier, 1, device_id={"dp": lax.rem(d + off, n)}, device_id_type=MESH)

    @pl.when(z > 0)
    def _():
        pl.semaphore_signal(barrier, 1, device_id={"seq": z - 1}, device_id_type=MESH)

    @pl.when(z < seq - 1)
    def _():
        pl.semaphore_signal(barrier, 1, device_id={"seq": z + 1}, device_id_type=MESH)

    def chunk(p):
        if depth % 128 == 0:
            return hid.at[:, pl.ds(pl.multiple_of(p * depth, 128), depth)]
        return hid.at[p]

    local = [
        pltpu.make_async_copy(chunk(d), hbuf.at[k, c], loc.at[0]),
        pltpu.make_async_copy(weight, wv, loc.at[1]),
        pltpu.make_async_copy(query, qv, loc.at[2]),
        pltpu.make_async_copy(cot, cv, loc.at[3]),
    ] + [
        pltpu.make_async_copy(keys.at[:, pl.ds(gi * cols, cols)], kwin.at[gi, back], loc.at[5 + gi])
        for gi in range(PARTS)
    ]
    for copy in local:
        copy.start()
    inner = jnp.logical_and(z > 0, z < seq - 1)
    pl.semaphore_wait(barrier, n - 1 + jnp.where(inner, 2, 1))

    def key_hop(gi, s):
        src = keys.at[:, pl.ds(gi * cols, cols)] if s == 1 else kwin.at[gi, back - s + 1]
        cond = jnp.logical_and(z < seq - 1, z - s + 1 >= 0)
        start(remote(
            src, kwin.at[gi, back - s], ks.at[gi, s - 1], kr.at[gi, s - 1], seq=z + 1
        ), cond)

    def key_land(gi, s):
        @pl.when(z - s >= 0)
        def _():
            remote(
                kwin.at[gi, back - s], kwin.at[gi, back - s],
                ks.at[gi, s - 1], kr.at[gi, s - 1], seq=z,
            ).wait_recv()

    def keys_on(gi):
        for s in range(2, back + 1):
            key_land(gi, s - 1)
            key_hop(gi, s)

    for gi in range(PARTS):
        key_hop(gi, 1)
    for off in range(n - 1, 0, -1):
        p = lax.rem(d + off, n)
        start(remote(chunk(p), hbuf.at[k, c], hs.at[off], hr.at[k, c], dp=p))

    def hidden_land(kk):
        for cc in range(chips):
            @pl.when(jnp.logical_or(cc != c, kk != k))
            def _():
                remote(hbuf.at[kk, cc], hbuf.at[kk, cc], hs.at[0], hr.at[kk, cc], dp=d).wait_recv()

    def partial_values(kk, gi):
        rows = hbuf[kk].reshape(chips * tok, depth)
        got = mm(rows, wv[:, gi * cols:(gi + 1) * cols])
        pbuf[gi, kk] = got.astype(BF).reshape(chips, tok, cols)

    def values_pair():
        local[0].wait()
        local[1].wait()
        hidden_land(other)
        for gi in range(PARTS):
            partial_values(other, gi)
            start(remote(pbuf.at[gi, other], prec.at[gi], ps.at[gi], pr.at[gi], dp=partner))

    def values_own():
        hidden_land(k)
        for gi in range(PARTS):
            partial_values(k, gi)

    def values_send(gi):
        remote(pbuf.at[gi, k], prec.at[gi], ps.at[gi], pr.at[gi], dp=partner).wait_recv()
        csum[gi] = (pbuf[gi, k].astype(F32) + prec[gi].astype(F32)).astype(BF)
        for co in range(1, chips):
            cc = lax.rem(c + co, chips)
            start(remote(
                csum.at[gi, cc], vrec.at[gi, c], vs.at[gi, co], vr.at[gi, c], dp=cc * 2 + k
            ))

    def turn_hidden():
        for kk in range(2):
            for cc in range(chips):
                ht[:, (kk * chips + cc) * tok:(kk * chips + cc + 1) * tok] = hbuf[kk, cc].T

    def value_hop(gi, s):
        cond = jnp.logical_and(z < seq - 1, z - s + 1 >= 0)
        start(remote(
            vwin.at[gi, back - s + 1], vwin.at[gi, back - s],
            vcs.at[gi, s - 1], vcr.at[gi, s - 1], seq=z + 1,
        ), cond)

    def value_land(gi, s):
        @pl.when(z - s >= 0)
        def _():
            remote(
                vwin.at[gi, back - s], vwin.at[gi, back - s],
                vcs.at[gi, s - 1], vcr.at[gi, s - 1], seq=z,
            ).wait_recv()

    def values_done(gi):
        total = csum[gi, c].astype(F32)
        for co in range(1, chips):
            cc = lax.rem(c + co, chips)
            remote(
                vrec.at[gi, cc], vrec.at[gi, cc], vs.at[gi, 0], vr.at[gi, cc], dp=d
            ).wait_recv()
            total += vrec[gi, cc].astype(F32)
        vwin[gi, back] = total.astype(BF)
        value_hop(gi, 1)

    def values_on(gi):
        for s in range(2, back + 1):
            value_land(gi, s - 1)
            value_hop(gi, s)

    def pair_rows(j, pair):
        at = [slice((j * GROUP + pair * 2 + h) * HEAD_DIM, (j * GROUP + pair * 2 + h + 1) * HEAD_DIM)
              for h in range(2)]
        qp = jnp.concatenate([qv[:, a] for a in at], axis=0)
        cp = jnp.concatenate([cv[:, a] for a in at], axis=0)
        return at, qp, cp

    def scores(gi):
        local[5 + gi - 1].wait()
        key_land(gi, back)
        key_at = (z - back) * tok + lax.broadcasted_iota(jnp.int32, (window, tok), 0)
        query_at = z * tok + lax.broadcasted_iota(jnp.int32, (window, tok), 1)
        own_at = z * tok + lax.broadcasted_iota(jnp.int32, (1, tok), 1)
        first = jnp.zeros((1, tok), jnp.int32)
        end = 0
        for r in range(lengths.shape[1] - 1):
            end = end + lengths[0, r]
            first = jnp.where(own_at >= end, end, first)
        mask = jnp.logical_and(key_at >= first, key_at <= query_at)
        bias = jnp.where(mask, 0.0, -1e30).astype(F32)
        bias = jnp.concatenate([bias, bias], axis=1)
        for jl in range(heads_per):
            j = gi * heads_per + jl
            lcol = slice(jl * HEAD_DIM, (jl + 1) * HEAD_DIM)
            kj = kwin[gi, :, :, lcol].reshape(window, HEAD_DIM)
            dvj = jnp.zeros((window, HEAD_DIM), F32)
            for pair in range(GROUP // 2):
                at, qp, cp = pair_rows(j, pair)
                st = mm(kj, qp, NT) * (SCALE * math.log2(math.e)) + bias
                e = jnp.exp2(st - jnp.max(st, axis=0, keepdims=True))
                pb = (e * (1.0 / jnp.sum(e, axis=0, keepdims=True))).astype(BF)
                probs[j, pair] = pb
                dvj += mm(pb, cp)
            dpart[0, gi, :, :, lcol] = dvj.reshape(back + 1, tok, HEAD_DIM)
        grad_step(0, gi, 0)

    def through(j):
        gi, jl = divmod(j, heads_per)
        if jl == 0:
            value_land(gi, back)
        lcol = slice(jl * HEAD_DIM, (jl + 1) * HEAD_DIM)
        kt = kwin[gi, :, :, lcol].reshape(window, HEAD_DIM).T
        vj = vwin[gi, :, :, lcol].reshape(window, HEAD_DIM)
        vt = vj.T
        dkj = jnp.zeros((window, HEAD_DIM), F32)
        for pair in range(GROUP // 2):
            at, qp, cp = pair_rows(j, pair)
            pb = probs[j, pair]
            p = pb.astype(F32)
            dp = mm(vj, cp, NT)
            delta = jnp.sum(p * dp, axis=0, keepdims=True)
            sg = (p * (dp - delta)).astype(BF)
            dkj += mm(sg, qp)
            ot = mm(vt, pb).astype(BF)
            qt = (mm(kt, sg) * SCALE).astype(BF)
            for h in range(2):
                part = slice(h * HEAD_DIM, (h + 1) * HEAD_DIM)
                ov[:, at[h]] = ot[:, part].T
                dqv[:, at[h]] = qt[:, part].T
        dpart[1, gi, :, :, lcol] = (dkj * SCALE).reshape(back + 1, tok, HEAD_DIM)
        if jl == heads_per - 1:
            grad_step(1, gi, 0)
            wide = heads_per * GROUP * HEAD_DIM
            mine = pl.ds(gi * wide, wide)
            for index, (a, b) in enumerate(((ov, out), (dqv, dq))):
                copy = pltpu.make_async_copy(a.at[:, mine], b.at[:, mine], osem.at[gi, index])
                copy.start()
                pending.append((None, copy))

    def grad_copy(w, gi, i):
        return remote(
            dsend.at[w, gi, i], drec.at[w, gi, i], ds_.at[w, gi, i], dr.at[w, gi, i], seq=z - 1
        )

    def grad_step(w, gi, i):
        if i >= 1:
            @pl.when(jnp.logical_and(z < seq - 1, z - back + i >= 0))
            def _():
                grad_copy(w, gi, i - 1).wait_recv()
                dpart[w, gi, i] += drec[w, gi, i - 1].astype(F32)
        if i < back:
            dsend[w, gi, i] = dpart[w, gi, i].astype(BF)
            start(grad_copy(w, gi, i), z - back + i >= 0)

    def gather_send(gi):
        grad_step(0, gi, back)
        dvall[gi, k, c] = dpart[0, gi, back].astype(BF)
        for co in range(1, chips):
            cc = lax.rem(c + co, chips)
            start(remote(
                dvall.at[gi, k, c], dvall.at[gi, k, c], gs.at[gi, co], gr.at[gi, k, c], dp=cc * 2 + k
            ))
        start(remote(
            dvall.at[gi, k, c], dvall.at[gi, k, c], fs.at[gi, 0], gr.at[gi, k, c], dp=partner
        ))

    def key_grads(gi):
        grad_step(1, gi, back)
        dk[:, gi * cols:(gi + 1) * cols] = dpart[1, gi, back].astype(BF)

    def gather_land(gi, kk, cc):
        remote(
            dvall.at[gi, kk, cc], dvall.at[gi, kk, cc], gs.at[gi, 0], gr.at[gi, kk, cc], dp=d
        ).wait_recv()

    def gather_on(gi):
        for co in range(1, chips):
            cc = lax.rem(c + co, chips)
            gather_land(gi, k, cc)
            start(remote(
                dvall.at[gi, k, cc], dvall.at[gi, k, cc], fs.at[gi, co], gr.at[gi, k, cc], dp=partner
            ))

    half = seq // 2
    low = z < half
    inward = jnp.where(low, z + 1, z - 1)
    outward = jnp.where(low, z - 1, z + 1)
    middle = jnp.logical_or(z == half - 1, z == half)
    edge = jnp.logical_or(z == 0, z == seq - 1)
    not_middle = jnp.logical_not(middle)
    not_edge = jnp.logical_not(edge)
    cut = depth // AR_CUTS

    def weight_grad(gi):
        for cc in range(chips):
            gather_land(gi, other, cc)
        rows = dvall[gi].reshape(n * tok, cols)
        dwv[gi] = mm(ht[...], rows)
        for r in range(AR_CUTS):
            reduce_in(gi, r, True)

    def reduce_in(gi, r, first):
        at = (gi, pl.ds(r * cut, cut))

        def send():
            msg[at] = dwv[at].astype(BF)

        if first:
            @pl.when(edge)
            def _():
                send()
            cond = edge
        else:
            @pl.when(not_edge)
            def _():
                remote(msg.at[at], rec_out.at[at], ais.at[gi, r], aor.at[gi, r], seq=z).wait_recv()
                dwv[at] += rec_out[at].astype(F32)
                send()
            cond = not_edge
        a = jnp.logical_and(cond, not_middle)
        b = jnp.logical_and(cond, middle)
        start(remote(msg.at[at], rec_out.at[at], ais.at[gi, r], aor.at[gi, r], seq=inward), a)
        start(remote(msg.at[at], rec_in.at[at], ais.at[gi, r], air.at[gi, r], seq=inward), b)

    def reduce_out(gi, r):
        at = (gi, pl.ds(r * cut, cut))
        remote(msg.at[at], rec_in.at[at], ais.at[gi, r], air.at[gi, r], seq=z).wait_recv()

        @pl.when(middle)
        def _():
            tot[at] = (msg[at].astype(F32) + rec_in[at].astype(F32)).astype(BF)

        @pl.when(not_middle)
        def _():
            tot[at] = rec_in[at]

        start(remote(tot.at[at], rec_in.at[at], aos.at[gi, r], air.at[gi, r], seq=outward), not_edge)
        dwv[at] = tot[at].astype(F32)
        copy = pltpu.make_async_copy(
            dwv.at[at], dw.at[pl.ds(r * cut, cut), pl.ds(gi * cols, cols)], dwsem.at[gi, r]
        )
        copy.start()
        pending.append((None, copy))

    def block(p):
        if depth % 128 == 0:
            return ig.at[:, pl.ds(pl.multiple_of(p * depth, 128), depth)]
        return ig.at[p]

    def input_grad(gi):
        rows = dvall[gi].reshape(n * tok, cols)
        got = mm(rows, wv[:, gi * cols:(gi + 1) * cols], NT)
        if gi == 0:
            igacc[...] = got
        elif gi < PARTS - 1:
            igacc[...] += got
        else:
            igs[...] = (igacc[...] + got).astype(BF).reshape(2, chips, tok, depth)
            for off in range(1, n):
                p = lax.rem(d + off, n)
                start(remote(
                    igs.at[lax.rem(p, 2), lax.div(p, 2)], block(d),
                    igss.at[off], igr.at[k, c], dp=p,
                ))
            copy = pltpu.make_async_copy(igs.at[k, c], block(d), loc.at[4])
            copy.start()
            pending.append((None, copy))

    def grads_on(w, gi):
        for i in range(1, back):
            grad_step(w, gi, i)

    def value_grads_on(gi):
        grads_on(0, gi)

    def key_grads_on(gi):
        grads_on(1, gi)

    def reduces(gi):
        for r in range(AR_CUTS):
            reduce_in(gi, r, False)

    def finish(gi):
        for r in range(AR_CUTS):
            reduce_out(gi, r)

    def later(*rows):
        for row in rows:
            for at in range(0, len(row), 2):
                row[at](row[at + 1])

    local[2].wait()
    local[3].wait()
    later(
        (keys_on, 0, keys_on, 1, keys_on, 2),
        (scores, 0, keys_on, 3),
        (scores, 1, value_grads_on, 0),
    )
    values_pair()
    later((scores, 2, value_grads_on, 1, gather_send, 0))
    values_own()
    for gi in range(PARTS):
        values_send(gi)
    later((scores, 3, value_grads_on, 2, gather_send, 1))
    turn_hidden()
    later(
        (value_grads_on, 3, gather_send, 2, values_done, 0, gather_send, 3),
        (values_done, 1, gather_on, 0, values_on, 0, values_done, 2, values_on, 1),
        (weight_grad, 0, gather_on, 1, through, 0),
        (values_done, 3, values_on, 2, weight_grad, 1, gather_on, 2, through, 1),
        (values_on, 3, reduces, 0, weight_grad, 2, gather_on, 3, through, 2),
        (reduces, 1, weight_grad, 3),
        (input_grad, 0, input_grad, 1, input_grad, 2, input_grad, 3),
        (through, 3, finish, 0, reduces, 2, through, 4),
        (finish, 1, reduces, 3, through, 5, key_grads_on, 0, through, 6),
        (finish, 2, key_grads_on, 1, through, 7),
        (key_grads_on, 2, key_grads, 0, finish, 3, key_grads_on, 3),
        (key_grads, 1, key_grads, 2, key_grads, 3),
    )

    for off in range(1, n):
        p = lax.rem(d + off, n)
        slot = (lax.rem(p, 2), lax.div(p, 2))
        remote(igs.at[slot], block(p), igss.at[0], igr.at[slot], dp=d).wait_recv()
    for cond, copy in pending:
        if hasattr(copy, "wait_send") and copy.is_remote:
            when(cond, lambda copy=copy: copy.wait_send())
        else:
            copy.wait()


def body(hidden_states, value_weight, query_states, key_states, cotangent, lengths, n, seq):
    tok, width = hidden_states.shape
    depth = value_weight.shape[0]
    kv_cols = value_weight.shape[1]
    cols = kv_cols // PARTS
    chips = n // 2
    packed = tok * seq
    back = -(-(packed // 2 - 1) // tok)
    hid = hidden_states
    aligned = depth % 128 == 0
    if not aligned:
        hid = hid.reshape(tok, n, depth).transpose(1, 0, 2)
    vmem = pl.BlockSpec(memory_space=pltpu.VMEM)
    hbm = pl.BlockSpec(memory_space=pl.ANY)
    dma = pltpu.SemaphoreType.DMA
    out, dq, dk, ig, dw = pl.pallas_call(
        functools.partial(kernel, n, seq, back, tok, depth),
        out_shape=(
            jax.ShapeDtypeStruct(query_states.shape, BF),
            jax.ShapeDtypeStruct(query_states.shape, BF),
            jax.ShapeDtypeStruct(key_states.shape, BF),
            jax.ShapeDtypeStruct((tok, width) if aligned else (n, tok, depth), BF),
            jax.ShapeDtypeStruct((depth, kv_cols), F32),
        ),
        in_specs=[pl.BlockSpec(memory_space=pltpu.SMEM), hbm, hbm, hbm, hbm, hbm],
        out_specs=(hbm, hbm, vmem, hbm, hbm),
        scratch_shapes=[
            pltpu.VMEM((2, chips, tok, depth), BF),
            pltpu.VMEM((depth, n * tok), BF),
            pltpu.VMEM((depth, kv_cols), BF),
            pltpu.VMEM(query_states.shape, BF),
            pltpu.VMEM(query_states.shape, BF),
            pltpu.VMEM(query_states.shape, BF),
            pltpu.VMEM(query_states.shape, BF),
            pltpu.VMEM((PARTS, back + 1, tok, cols), BF),
            pltpu.VMEM((PARTS, back + 1, tok, cols), BF),
            pltpu.VMEM((KV_HEADS, GROUP // 2, (back + 1) * tok, 2 * tok), BF),
            pltpu.VMEM((PARTS, 2, chips, tok, cols), BF),
            pltpu.VMEM((PARTS, chips, tok, cols), BF),
            pltpu.VMEM((PARTS, chips, tok, cols), BF),
            pltpu.VMEM((PARTS, chips, tok, cols), BF),
            pltpu.VMEM((2, PARTS, back + 1, tok, cols), F32),
            pltpu.VMEM((2, PARTS, back, tok, cols), BF),
            pltpu.VMEM((2, PARTS, back, tok, cols), BF),
            pltpu.VMEM((PARTS, 2, chips, tok, cols), BF),
            pltpu.VMEM((n * tok, depth), F32),
            pltpu.VMEM((2, chips, tok, depth), BF),
            pltpu.VMEM((PARTS, depth, cols), F32),
            pltpu.VMEM((PARTS, depth, cols), BF),
            pltpu.VMEM((PARTS, depth, cols), BF),
            pltpu.VMEM((PARTS, depth, cols), BF),
            pltpu.VMEM((PARTS, depth, cols), BF),
            dma((5 + PARTS,)),
            dma((n,)), dma((2, chips)),
            dma((PARTS, back)), dma((PARTS, back)),
            dma((PARTS,)), dma((PARTS,)),
            dma((PARTS, chips)), dma((PARTS, chips)),
            dma((PARTS, back)), dma((PARTS, back)),
            dma((2, PARTS, back)), dma((2, PARTS, back)),
            dma((PARTS, chips)), dma((PARTS, 2, chips)),
            dma((PARTS, chips)), dma((1,)),
            dma((n,)), dma((2, chips)),
            dma((PARTS, AR_CUTS)), dma((PARTS, AR_CUTS)),
            dma((PARTS, AR_CUTS)), dma((PARTS, AR_CUTS)),
            dma((PARTS, 2)), dma((PARTS, AR_CUTS)),
        ],
        compiler_params=pltpu.CompilerParams(
            collective_id=0, has_side_effects=True, vmem_limit_bytes=60 * 1024 * 1024
        ),
    )(lengths, hid, value_weight, query_states, key_states, cotangent)
    if not aligned:
        ig = ig.transpose(1, 0, 2).reshape(tok, width)
    return out, dq, dk, ig, dw


def solution(mesh):
    rows = P(("dp", "seq"), None)
    placed = (rows, P("dp", None), rows, rows, rows, P("dp", None))
    return jax.shard_map(
        functools.partial(body, n=mesh.shape["dp"], seq=mesh.shape["seq"]),
        mesh=mesh,
        in_specs=placed,
        out_specs=(rows, rows, rows, rows, P("dp", None)),
        check_vma=False,
    )
```

```python
import functools
import math

import jax
import jax.numpy as jnp
from jax import lax
from jax.experimental import pallas as pl
from jax.experimental.pallas import tpu as pltpu
from jax.sharding import PartitionSpec as P

HEADS = 64
KV_HEADS = 8
HEAD_DIM = 128
GROUP = HEADS // KV_HEADS
SCALE = HEAD_DIM ** (-0.5)
MESH = pl.DeviceIdType.MESH
BF = jnp.bfloat16
F32 = jnp.float32
PARTS = 4
AR_CUTS = 2

NT = (((1,), (1,)), ((), ()))


def mm(a, b, dims=(((1,), (0,)), ((), ()))):
    return lax.dot_general(a, b, dims, preferred_element_type=F32)


def kernel(
    n, seq, back, tok, depth, lengths, hid, weight, query, keys, cot,
    out, dq, dk, ig, dw,
    hbuf, ht, wv, qv, cv, ov, dqv, kwin, vwin, probs, pbuf, prec, csum, vrec,
    dpart, dsend, drec, dvall, igacc, igs, dwv, msg, rec_out, rec_in, tot,
    loc, hs, hr, ks, kr, ps, pr, vs, vr, vcs, vcr, ds_, dr, gs, gr, fs, fr, igss, igr,
    ais, air, aos, aor, osem, dwsem,
):
    chips = n // 2
    kv_cols = KV_HEADS * HEAD_DIM
    cols = kv_cols // PARTS
    heads_per = KV_HEADS // PARTS
    window = (back + 1) * tok
    d = lax.axis_index("dp")
    z = lax.axis_index("seq")
    c = lax.div(d, 2)
    k = lax.rem(d, 2)
    other = 1 - k
    partner = c * 2 + other
    pending = []

    def remote(src, dst, ssem, rsem, **where):
        return pltpu.make_async_remote_copy(
            src_ref=src, dst_ref=dst, send_sem=ssem, recv_sem=rsem,
            device_id=where, device_id_type=MESH,
        )

    def when(cond, fn):
        if cond is None:
            fn()
        else:
            pl.when(cond)(fn)

    def start(copy, cond=None):
        when(cond, lambda: copy.start())
        pending.append((cond, copy))

    kwin[:, pl.ds(0, back)] = jnp.zeros((PARTS, back, tok, cols), BF)
    vwin[:, pl.ds(0, back)] = jnp.zeros((PARTS, back, tok, cols), BF)

    barrier = pltpu.get_barrier_semaphore()
    for off in range(1, n):
        pl.semaphore_signal(barrier, 1, device_id={"dp": lax.rem(d + off, n)}, device_id_type=MESH)

    @pl.when(z > 0)
    def _():
        pl.semaphore_signal(barrier, 1, device_id={"seq": z - 1}, device_id_type=MESH)

    @pl.when(z < seq - 1)
    def _():
        pl.semaphore_signal(barrier, 1, device_id={"seq": z + 1}, device_id_type=MESH)

    def chunk(p):
        if depth % 128 == 0:
            return hid.at[:, pl.ds(pl.multiple_of(p * depth, 128), depth)]
        return hid.at[p]

    local = [
        pltpu.make_async_copy(chunk(d), hbuf.at[k, c], loc.at[0]),
        pltpu.make_async_copy(weight, wv, loc.at[1]),
        pltpu.make_async_copy(query, qv, loc.at[2]),
        pltpu.make_async_copy(cot, cv, loc.at[3]),
    ] + [
        pltpu.make_async_copy(keys.at[:, pl.ds(gi * cols, cols)], kwin.at[gi, back], loc.at[5 + gi])
        for gi in range(PARTS)
    ]
    for copy in local:
        copy.start()
    inner = jnp.logical_and(z > 0, z < seq - 1)
    pl.semaphore_wait(barrier, n - 1 + jnp.where(inner, 2, 1))

    def key_hop(gi, s):
        src = keys.at[:, pl.ds(gi * cols, cols)] if s == 1 else kwin.at[gi, back - s + 1]
        cond = jnp.logical_and(z < seq - 1, z - s + 1 >= 0)
        start(remote(
            src, kwin.at[gi, back - s], ks.at[gi, s - 1], kr.at[gi, s - 1], seq=z + 1
        ), cond)

    def key_land(gi, s):
        @pl.when(z - s >= 0)
        def _():
            remote(
                kwin.at[gi, back - s], kwin.at[gi, back - s],
                ks.at[gi, s - 1], kr.at[gi, s - 1], seq=z,
            ).wait_recv()

    def keys_on(gi):
        for s in range(2, back + 1):
            key_land(gi, s - 1)
            key_hop(gi, s)

    for gi in range(PARTS):
        key_hop(gi, 1)
    for off in range(n - 1, 0, -1):
        p = lax.rem(d + off, n)
        start(remote(chunk(p), hbuf.at[k, c], hs.at[off], hr.at[k, c], dp=p))

    def hidden_land(kk):
        for cc in range(chips):
            @pl.when(jnp.logical_or(cc != c, kk != k))
            def _():
                remote(hbuf.at[kk, cc], hbuf.at[kk, cc], hs.at[0], hr.at[kk, cc], dp=d).wait_recv()

    def partial_values(kk, gi):
        rows = hbuf[kk].reshape(chips * tok, depth)
        got = mm(rows, wv[:, gi * cols:(gi + 1) * cols])
        pbuf[gi, kk] = got.astype(BF).reshape(chips, tok, cols)

    def values_pair():
        local[0].wait()
        local[1].wait()
        hidden_land(other)
        for gi in range(PARTS):
            partial_values(other, gi)
            start(remote(pbuf.at[gi, other], prec.at[gi], ps.at[gi], pr.at[gi], dp=partner))

    def values_own():
        hidden_land(k)
        for gi in range(PARTS):
            partial_values(k, gi)

    def values_send(gi):
        remote(pbuf.at[gi, k], prec.at[gi], ps.at[gi], pr.at[gi], dp=partner).wait_recv()
        csum[gi] = (pbuf[gi, k].astype(F32) + prec[gi].astype(F32)).astype(BF)
        for co in range(1, chips):
            cc = lax.rem(c + co, chips)
            start(remote(
                csum.at[gi, cc], vrec.at[gi, c], vs.at[gi, co], vr.at[gi, c], dp=cc * 2 + k
            ))

    def turn_hidden():
        for kk in range(2):
            for cc in range(chips):
                ht[:, (kk * chips + cc) * tok:(kk * chips + cc + 1) * tok] = hbuf[kk, cc].T

    def value_hop(gi, s):
        cond = jnp.logical_and(z < seq - 1, z - s + 1 >= 0)
        start(remote(
            vwin.at[gi, back - s + 1], vwin.at[gi, back - s],
            vcs.at[gi, s - 1], vcr.at[gi, s - 1], seq=z + 1,
        ), cond)

    def value_land(gi, s):
        @pl.when(z - s >= 0)
        def _():
            remote(
                vwin.at[gi, back - s], vwin.at[gi, back - s],
                vcs.at[gi, s - 1], vcr.at[gi, s - 1], seq=z,
            ).wait_recv()

    def values_done(gi):
        total = csum[gi, c].astype(F32)
        for co in range(1, chips):
            cc = lax.rem(c + co, chips)
            remote(
                vrec.at[gi, cc], vrec.at[gi, cc], vs.at[gi, 0], vr.at[gi, cc], dp=d
            ).wait_recv()
            total += vrec[gi, cc].astype(F32)
        vwin[gi, back] = total.astype(BF)
        value_hop(gi, 1)

    def values_on(gi):
        for s in range(2, back + 1):
            value_land(gi, s - 1)
            value_hop(gi, s)

    def pair_rows(j, pair):
        at = [slice((j * GROUP + pair * 2 + h) * HEAD_DIM, (j * GROUP + pair * 2 + h + 1) * HEAD_DIM)
              for h in range(2)]
        qp = jnp.concatenate([qv[:, a] for a in at], axis=0)
        cp = jnp.concatenate([cv[:, a] for a in at], axis=0)
        return at, qp, cp

    def scores(gi):
        local[5 + gi - 1].wait()
        key_land(gi, back)
        key_at = (z - back) * tok + lax.broadcasted_iota(jnp.int32, (window, tok), 0)
        query_at = z * tok + lax.broadcasted_iota(jnp.int32, (window, tok), 1)
        own_at = z * tok + lax.broadcasted_iota(jnp.int32, (1, tok), 1)
        first = jnp.zeros((1, tok), jnp.int32)
        end = 0
        for r in range(lengths.shape[1] - 1):
            end = end + lengths[0, r]
            first = jnp.where(own_at >= end, end, first)
        mask = jnp.logical_and(key_at >= first, key_at <= query_at)
        bias = jnp.where(mask, 0.0, -1e30).astype(F32)
        bias = jnp.concatenate([bias, bias], axis=1)
        for jl in range(heads_per):
            j = gi * heads_per + jl
            lcol = slice(jl * HEAD_DIM, (jl + 1) * HEAD_DIM)
            kj = kwin[gi, :, :, lcol].reshape(window, HEAD_DIM)
            dvj = jnp.zeros((window, HEAD_DIM), F32)
            for pair in range(GROUP // 2):
                at, qp, cp = pair_rows(j, pair)
                st = mm(kj, qp, NT) * (SCALE * math.log2(math.e)) + bias
                e = jnp.exp2(st - jnp.max(st, axis=0, keepdims=True))
                pb = (e * (1.0 / jnp.sum(e, axis=0, keepdims=True))).astype(BF)
                probs[j, pair] = pb
                dvj += mm(pb, cp)
            dpart[0, gi, :, :, lcol] = dvj.reshape(back + 1, tok, HEAD_DIM)
        grad_step(0, gi, 0)

    def through(j):
        gi, jl = divmod(j, heads_per)
        if jl == 0:
            value_land(gi, back)
        lcol = slice(jl * HEAD_DIM, (jl + 1) * HEAD_DIM)
        kt = kwin[gi, :, :, lcol].reshape(window, HEAD_DIM).T
        vj = vwin[gi, :, :, lcol].reshape(window, HEAD_DIM)
        vt = vj.T
        dkj = jnp.zeros((window, HEAD_DIM), F32)
        for pair in range(GROUP // 2):
            at, qp, cp = pair_rows(j, pair)
            pb = probs[j, pair]
            p = pb.astype(F32)
            dp = mm(vj, cp, NT)
            delta = jnp.sum(p * dp, axis=0, keepdims=True)
            sg = (p * (dp - delta)).astype(BF)
            dkj += mm(sg, qp)
            ot = mm(vt, pb).astype(BF)
            qt = (mm(kt, sg) * SCALE).astype(BF)
            for h in range(2):
                part = slice(h * HEAD_DIM, (h + 1) * HEAD_DIM)
                ov[:, at[h]] = ot[:, part].T
                dqv[:, at[h]] = qt[:, part].T
        dpart[1, gi, :, :, lcol] = (dkj * SCALE).reshape(back + 1, tok, HEAD_DIM)
        if jl == heads_per - 1:
            grad_step(1, gi, 0)
            wide = heads_per * GROUP * HEAD_DIM
            mine = pl.ds(gi * wide, wide)
            for index, (a, b) in enumerate(((ov, out), (dqv, dq))):
                copy = pltpu.make_async_copy(a.at[:, mine], b.at[:, mine], osem.at[gi, index])
                copy.start()
                pending.append((None, copy))

    def grad_copy(w, gi, i):
        return remote(
            dsend.at[w, gi, i], drec.at[w, gi, i], ds_.at[w, gi, i], dr.at[w, gi, i], seq=z - 1
        )

    def grad_step(w, gi, i):
        if i >= 1:
            @pl.when(jnp.logical_and(z < seq - 1, z - back + i >= 0))
            def _():
                grad_copy(w, gi, i - 1).wait_recv()
                dpart[w, gi, i] += drec[w, gi, i - 1].astype(F32)
        if i < back:
            dsend[w, gi, i] = dpart[w, gi, i].astype(BF)
            start(grad_copy(w, gi, i), z - back + i >= 0)

    def gather_send(gi):
        grad_step(0, gi, back)
        dvall[gi, k, c] = dpart[0, gi, back].astype(BF)
        for co in range(1, chips):
            cc = lax.rem(c + co, chips)
            start(remote(
                dvall.at[gi, k, c], dvall.at[gi, k, c], gs.at[gi, co], gr.at[gi, k, c], dp=cc * 2 + k
            ))
        start(remote(
            dvall.at[gi, k, c], dvall.at[gi, k, c], fs.at[gi, 0], gr.at[gi, k, c], dp=partner
        ))

    def key_grads(gi):
        grad_step(1, gi, back)
        dk[:, gi * cols:(gi + 1) * cols] = dpart[1, gi, back].astype(BF)

    def gather_land(gi, kk, cc):
        remote(
            dvall.at[gi, kk, cc], dvall.at[gi, kk, cc], gs.at[gi, 0], gr.at[gi, kk, cc], dp=d
        ).wait_recv()

    def gather_on(gi):
        for co in range(1, chips):
            cc = lax.rem(c + co, chips)
            gather_land(gi, k, cc)
            start(remote(
                dvall.at[gi, k, cc], dvall.at[gi, k, cc], fs.at[gi, co], gr.at[gi, k, cc], dp=partner
            ))

    half = seq // 2
    low = z < half
    inward = jnp.where(low, z + 1, z - 1)
    outward = jnp.where(low, z - 1, z + 1)
    middle = jnp.logical_or(z == half - 1, z == half)
    edge = jnp.logical_or(z == 0, z == seq - 1)
    not_middle = jnp.logical_not(middle)
    not_edge = jnp.logical_not(edge)
    cut = depth // AR_CUTS

    def weight_grad(gi):
        for cc in range(chips):
            gather_land(gi, other, cc)
        rows = dvall[gi].reshape(n * tok, cols)
        dwv[gi] = mm(ht[...], rows)
        for r in range(AR_CUTS):
            reduce_in(gi, r, True)

    def reduce_in(gi, r, first):
        at = (gi, pl.ds(r * cut, cut))

        def send():
            msg[at] = dwv[at].astype(BF)

        if first:
            @pl.when(edge)
            def _():
                send()
            cond = edge
        else:
            @pl.when(not_edge)
            def _():
                remote(msg.at[at], rec_out.at[at], ais.at[gi, r], aor.at[gi, r], seq=z).wait_recv()
                dwv[at] += rec_out[at].astype(F32)
                send()
            cond = not_edge
        a = jnp.logical_and(cond, not_middle)
        b = jnp.logical_and(cond, middle)
        start(remote(msg.at[at], rec_out.at[at], ais.at[gi, r], aor.at[gi, r], seq=inward), a)
        start(remote(msg.at[at], rec_in.at[at], ais.at[gi, r], air.at[gi, r], seq=inward), b)

    def reduce_out(gi, r):
        at = (gi, pl.ds(r * cut, cut))
        remote(msg.at[at], rec_in.at[at], ais.at[gi, r], air.at[gi, r], seq=z).wait_recv()

        @pl.when(middle)
        def _():
            tot[at] = (msg[at].astype(F32) + rec_in[at].astype(F32)).astype(BF)

        @pl.when(not_middle)
        def _():
            tot[at] = rec_in[at]

        start(remote(tot.at[at], rec_in.at[at], aos.at[gi, r], air.at[gi, r], seq=outward), not_edge)
        dwv[at] = tot[at].astype(F32)
        copy = pltpu.make_async_copy(
            dwv.at[at], dw.at[pl.ds(r * cut, cut), pl.ds(gi * cols, cols)], dwsem.at[gi, r]
        )
        copy.start()
        pending.append((None, copy))

    def block(p):
        if depth % 128 == 0:
            return ig.at[:, pl.ds(pl.multiple_of(p * depth, 128), depth)]
        return ig.at[p]

    def input_grad(gi):
        rows = dvall[gi].reshape(n * tok, cols)
        got = mm(rows, wv[:, gi * cols:(gi + 1) * cols], NT)
        if gi == 0:
            igacc[...] = got
        elif gi < PARTS - 1:
            igacc[...] += got
        else:
            igs[...] = (igacc[...] + got).astype(BF).reshape(2, chips, tok, depth)
            for off in range(1, n):
                p = lax.rem(d + off, n)
                start(remote(
                    igs.at[lax.rem(p, 2), lax.div(p, 2)], block(d),
                    igss.at[off], igr.at[k, c], dp=p,
                ))
            copy = pltpu.make_async_copy(igs.at[k, c], block(d), loc.at[4])
            copy.start()
            pending.append((None, copy))

    def grads_on(w, gi):
        for i in range(1, back):
            grad_step(w, gi, i)

    def value_grads_on(gi):
        grads_on(0, gi)

    def key_grads_on(gi):
        grads_on(1, gi)

    def reduces(gi):
        for r in range(AR_CUTS):
            reduce_in(gi, r, False)

    def finish(gi):
        for r in range(AR_CUTS):
            reduce_out(gi, r)

    def later(*rows):
        for row in rows:
            for at in range(0, len(row), 2):
                row[at](row[at + 1])

    local[2].wait()
    local[3].wait()
    later(
        (keys_on, 0, keys_on, 1, keys_on, 2),
        (scores, 0, keys_on, 3),
        (scores, 1, value_grads_on, 0),
    )
    values_pair()
    later((scores, 2, value_grads_on, 1, gather_send, 0))
    values_own()
    for gi in range(PARTS):
        values_send(gi)
    later((scores, 3, value_grads_on, 2, gather_send, 1))
    turn_hidden()
    later(
        (value_grads_on, 3, gather_send, 2, values_done, 0, gather_send, 3),
        (gather_on, 0, weight_grad, 0, values_done, 1, values_on, 0, values_done, 2, values_on, 1),
        (through, 0, gather_on, 1, weight_grad, 1, values_done, 3, values_on, 2),
        (through, 1, reduces, 0, gather_on, 2, weight_grad, 2, values_on, 3),
        (through, 2, reduces, 1, gather_on, 3, weight_grad, 3),
        (input_grad, 0, input_grad, 1, input_grad, 2, input_grad, 3),
        (reduces, 2, through, 3, finish, 0, reduces, 3, through, 4, finish, 1),
        (through, 5, key_grads_on, 0, through, 6, finish, 2, key_grads_on, 1, through, 7),
        (key_grads_on, 2, key_grads, 0, finish, 3, key_grads_on, 3),
        (key_grads, 1, key_grads, 2, key_grads, 3),
    )

    for off in range(1, n):
        p = lax.rem(d + off, n)
        slot = (lax.rem(p, 2), lax.div(p, 2))
        remote(igs.at[slot], block(p), igss.at[0], igr.at[slot], dp=d).wait_recv()
    for cond, copy in pending:
        if hasattr(copy, "wait_send") and copy.is_remote:
            when(cond, lambda copy=copy: copy.wait_send())
        else:
            copy.wait()


def body(hidden_states, value_weight, query_states, key_states, cotangent, lengths, n, seq):
    tok, width = hidden_states.shape
    depth = value_weight.shape[0]
    kv_cols = value_weight.shape[1]
    cols = kv_cols // PARTS
    chips = n // 2
    packed = tok * seq
    back = -(-(packed // 2 - 1) // tok)
    hid = hidden_states
    aligned = depth % 128 == 0
    if not aligned:
        hid = hid.reshape(tok, n, depth).transpose(1, 0, 2)
    vmem = pl.BlockSpec(memory_space=pltpu.VMEM)
    hbm = pl.BlockSpec(memory_space=pl.ANY)
    dma = pltpu.SemaphoreType.DMA
    out, dq, dk, ig, dw = pl.pallas_call(
        functools.partial(kernel, n, seq, back, tok, depth),
        out_shape=(
            jax.ShapeDtypeStruct(query_states.shape, BF),
            jax.ShapeDtypeStruct(query_states.shape, BF),
            jax.ShapeDtypeStruct(key_states.shape, BF),
            jax.ShapeDtypeStruct((tok, width) if aligned else (n, tok, depth), BF),
            jax.ShapeDtypeStruct((depth, kv_cols), F32),
        ),
        in_specs=[pl.BlockSpec(memory_space=pltpu.SMEM), hbm, hbm, hbm, hbm, hbm],
        out_specs=(hbm, hbm, vmem, hbm, hbm),
        scratch_shapes=[
            pltpu.VMEM((2, chips, tok, depth), BF),
            pltpu.VMEM((depth, n * tok), BF),
            pltpu.VMEM((depth, kv_cols), BF),
            pltpu.VMEM(query_states.shape, BF),
            pltpu.VMEM(query_states.shape, BF),
            pltpu.VMEM(query_states.shape, BF),
            pltpu.VMEM(query_states.shape, BF),
            pltpu.VMEM((PARTS, back + 1, tok, cols), BF),
            pltpu.VMEM((PARTS, back + 1, tok, cols), BF),
            pltpu.VMEM((KV_HEADS, GROUP // 2, (back + 1) * tok, 2 * tok), BF),
            pltpu.VMEM((PARTS, 2, chips, tok, cols), BF),
            pltpu.VMEM((PARTS, chips, tok, cols), BF),
            pltpu.VMEM((PARTS, chips, tok, cols), BF),
            pltpu.VMEM((PARTS, chips, tok, cols), BF),
            pltpu.VMEM((2, PARTS, back + 1, tok, cols), F32),
            pltpu.VMEM((2, PARTS, back, tok, cols), BF),
            pltpu.VMEM((2, PARTS, back, tok, cols), BF),
            pltpu.VMEM((PARTS, 2, chips, tok, cols), BF),
            pltpu.VMEM((n * tok, depth), F32),
            pltpu.VMEM((2, chips, tok, depth), BF),
            pltpu.VMEM((PARTS, depth, cols), F32),
            pltpu.VMEM((PARTS, depth, cols), BF),
            pltpu.VMEM((PARTS, depth, cols), BF),
            pltpu.VMEM((PARTS, depth, cols), BF),
            pltpu.VMEM((PARTS, depth, cols), BF),
            dma((5 + PARTS,)),
            dma((n,)), dma((2, chips)),
            dma((PARTS, back)), dma((PARTS, back)),
            dma((PARTS,)), dma((PARTS,)),
            dma((PARTS, chips)), dma((PARTS, chips)),
            dma((PARTS, back)), dma((PARTS, back)),
            dma((2, PARTS, back)), dma((2, PARTS, back)),
            dma((PARTS, chips)), dma((PARTS, 2, chips)),
            dma((PARTS, chips)), dma((1,)),
            dma((n,)), dma((2, chips)),
            dma((PARTS, AR_CUTS)), dma((PARTS, AR_CUTS)),
            dma((PARTS, AR_CUTS)), dma((PARTS, AR_CUTS)),
            dma((PARTS, 2)), dma((PARTS, AR_CUTS)),
        ],
        compiler_params=pltpu.CompilerParams(
            collective_id=0, has_side_effects=True, vmem_limit_bytes=60 * 1024 * 1024
        ),
    )(lengths, hid, value_weight, query_states, key_states, cotangent)
    if not aligned:
        ig = ig.transpose(1, 0, 2).reshape(tok, width)
    return out, dq, dk, ig, dw


def solution(mesh):
    rows = P(("dp", "seq"), None)
    placed = (rows, P("dp", None), rows, rows, rows, P("dp", None))
    return jax.shard_map(
        functools.partial(body, n=mesh.shape["dp"], seq=mesh.shape["seq"]),
        mesh=mesh,
        in_specs=placed,
        out_specs=(rows, rows, rows, rows, P("dp", None)),
        check_vma=False,
    )
```
